32 devices in a mesh: ctx: 16 (over z, y, x), tp: 2 (over core).
Axes of the slice: x: 2, y: 2, z: 4, core: 2. Of those that a mesh axis runs over, the one named last changes fastest.
Arguments:
- tokens: bfloat16 [4096, 4096], P('ctx', 'tp'), may hold values from -6 to 6
- norm_gain: bfloat16 [4096], P('tp'), may hold values from 0.25 to 1.75
- doc_ids: int32 [4096], P('ctx'), may hold values from 0 to 3, never falling along the last dimension, each value on 1 to 3840 neighbouring positions
- q_weight: bfloat16 [4096, 4096], P('ctx', 'tp'), may hold values from -0.09375 to 0.09375
- k_weight: bfloat16 [4096, 1024], P('ctx', 'tp'), may hold values from -0.09375 to 0.09375
- v_weight: bfloat16 [4096, 1024], P('ctx', 'tp'), may hold values from -0.09375 to 0.09375
- o_weight: bfloat16 [4096, 4096], P('tp', 'ctx'), may hold values from -0.09375 to 0.09375
Outputs:
- mixed: bfloat16 [4096, 4096], P('ctx', 'tp')
The draws below stay inside these ranges and needn't reach their ends.
Inputs may be any that keep to these rules, and one draw needn't show every extreme that they name: `doc_ids`: non-decreasing along the sequence; each document is a run of at most 3840 tokens and one run has exactly 3840.
All inputs are finite; a program needn't handle non-finite values.
Results may differ from the reference program's by a relative error of at most 0.015.
Values may be sent and summed in bfloat16 or wider, within the bound.
A program may use at most 128 MiB of HBM per device.

```python
import math
import jax
import jax.numpy as jnp
import numpy as np
from jax import lax

D = 4096
HEADS = 32
KV_HEADS = 8
HEAD = 128
TOK_SHARD = 256
WIN = 16
TOKENS = 4096
DOC_MOST = 3840
DOCS = 4
N_CTX = 16
N_TP = 2


def draw_tokens(key, part):
    noise = jax.random.truncated_normal(jax.random.fold_in(key, 11), -6.0, 6.0, (TOKENS, D), jnp.float32)
    return noise.astype(jnp.bfloat16)


def draw_q_weight(key, part):
    noise = jax.random.truncated_normal(jax.random.fold_in(key, 17), -6.0, 6.0, (D, HEADS * HEAD), jnp.float32) / math.sqrt(D)
    return noise.astype(jnp.bfloat16)


def draw_k_weight(key, part):
    noise = jax.random.truncated_normal(jax.random.fold_in(key, 19), -6.0, 6.0, (D, KV_HEADS * HEAD), jnp.float32) / math.sqrt(D)
    return noise.astype(jnp.bfloat16)


def block_scale(stream_key, dims, pieces, low, largest):
    loudness = 1.0
    for dim, blocks in pieces:
        heights = jax.random.uniform(jax.random.fold_in(jax.random.fold_in(stream_key, 6), dim), (blocks,), jnp.float32, low / len(pieces), largest / len(pieces))
        loudness = loudness * jnp.repeat(jnp.exp(heights), dims[dim] // blocks).reshape((-1,) + (1,) * (len(dims) - 1 - dim))
    return loudness


def split_up(amount, total, most, skew):
    weights = [(1 << 20) // math.isqrt(grade ** skew) + 1 for grade in range(2, amount + 1)]
    surplus, holding = total - most - (amount - 1), [1] * (amount - 1)
    while surplus > 0:
        candidates = [i for i in range(amount - 1) if holding[i] < most]
        whole, budget = sum([weights[i] for i in candidates]), surplus
        for i in candidates:
            addition = min(most - holding[i], max(1, budget * weights[i] // whole), surplus)
            holding[i] = holding[i] + addition
            surplus = surplus - addition
    return np.array([most] + holding)


def uneven_parts(stream_key, number_of, total, most, slope):
    if number_of == 2:
        one = jax.random.randint(stream_key, (), max(1, total - most), min(most, total - 1) + 1)
        return jnp.stack([one, total - one])
    tallies = jnp.asarray(split_up(number_of, total, most, slope), jnp.int32)
    pairs = (number_of - 1) // 2
    giver, taker = tallies[1:1 + 2 * pairs:2], tallies[2:2 + 2 * pairs:2]
    room = jnp.minimum(giver - 1, most - taker)
    moved = jax.random.randint(jax.random.fold_in(stream_key, 1), (pairs,), 0, 1 << 20) % (room + 1)
    tallies = tallies.at[1:1 + 2 * pairs:2].set(giver - moved).at[2:2 + 2 * pairs:2].set(taker + moved)
    return tallies[jax.random.permutation(jax.random.fold_in(stream_key, 2), number_of)]


def normal_values(key, extent, width, most, cuts=(), kind=jnp.bfloat16):
    loudness = block_scale(key, extent, cuts, -0.22, 0.18) if cuts else 1.0
    values = jax.random.normal(key, extent, jnp.float32) * width * loudness
    return jnp.minimum(jnp.maximum(values, -most), most).astype(kind)


def setup_inputs(seed: int = 0) -> dict:
    arg_keys = jax.random.split(jax.random.key(seed), 8)
    tokens = draw_tokens(jax.random.fold_in(arg_keys[7], 71), 0)
    norm_gain = jnp.clip(1.0 + 0.15 * jax.random.normal(arg_keys[1], (D,), jnp.float32), 0.25, 1.75).astype(jnp.bfloat16)
    doc_ids = jnp.searchsorted(jnp.cumsum(uneven_parts(arg_keys[2], DOCS, TOKENS, DOC_MOST, 2)), jnp.arange(TOKENS), side="right").astype(jnp.int32)
    q_weight = draw_q_weight(jax.random.fold_in(arg_keys[7], 71), 0)
    k_weight = draw_k_weight(jax.random.fold_in(arg_keys[7], 71), 0)
    v_weight = normal_values(arg_keys[5], (D, KV_HEADS * HEAD), D ** -0.5, 0.09375, ((0, 16), (1, 2)))
    o_weight = normal_values(arg_keys[6], (HEADS * HEAD, D), (HEADS * HEAD) ** -0.5, 0.09375, ((0, 2), (1, 16)))
    return {"tokens": tokens, "norm_gain": norm_gain, "doc_ids": doc_ids, "q_weight": q_weight, "k_weight": k_weight, "v_weight": v_weight, "o_weight": o_weight}


def rotate(values, positions):
    half_dim = values.shape[-1] // 2
    inv_freq = 500000.0 ** (-(jnp.arange(half_dim, dtype=jnp.float32) * 2.0) / values.shape[-1])
    angles = positions[:, None] * inv_freq[None, :]
    cos_part = jnp.cos(angles)[:, None, :]
    sin_part = jnp.sin(angles)[:, None, :]
    first_half = values[..., :half_dim]
    second_half = values[..., half_dim:]
    return jnp.concatenate([first_half * cos_part - second_half * sin_part, second_half * cos_part + first_half * sin_part], axis=-1)

def reference(tokens, norm_gain, doc_ids, q_weight, k_weight, v_weight, o_weight):
    x_float = tokens.astype(jnp.float32)
    mean_sq = lax.optimization_barrier(jnp.mean(x_float * x_float, axis=-1, keepdims=True))
    normed = (x_float * lax.rsqrt(mean_sq + 1e-05) * norm_gain.astype(jnp.float32)).astype(jnp.bfloat16)
    query = jnp.dot(normed, q_weight, preferred_element_type=jnp.float32)
    key = jnp.dot(normed, k_weight, preferred_element_type=jnp.float32)
    value = jnp.dot(normed, v_weight, preferred_element_type=jnp.float32)
    positions = jnp.arange(TOKENS, dtype=jnp.int32).astype(jnp.float32)
    group_size = HEADS // KV_HEADS
    q_rot = rotate(query.reshape(TOKENS, HEADS, HEAD), positions).astype(jnp.bfloat16)
    k_rot = rotate(key.reshape(TOKENS, KV_HEADS, HEAD), positions).astype(jnp.bfloat16)
    v_low = value.astype(jnp.bfloat16).reshape(TOKENS, KV_HEADS, HEAD)
    lead = (WIN - 1) * TOK_SHARD
    k_pad = jnp.concatenate([jnp.zeros((lead, KV_HEADS, HEAD), jnp.bfloat16), k_rot], axis=0)
    v_pad = jnp.concatenate([jnp.zeros((lead, KV_HEADS, HEAD), jnp.bfloat16), v_low], axis=0)
    doc_pad = jnp.concatenate([jnp.full((lead,), -1, jnp.int32), doc_ids.astype(jnp.int32)], axis=0)
    scale = 1.0 / HEAD ** 0.5

    def one_shard(shard):
        first_row = (shard * TOK_SHARD).astype(jnp.int32)
        q_block = lax.dynamic_slice_in_dim(q_rot, first_row, TOK_SHARD, 0).astype(jnp.float32)
        q_block = q_block.reshape(TOK_SHARD, KV_HEADS, group_size, HEAD)
        q_docs = lax.dynamic_slice_in_dim(doc_ids.astype(jnp.int32), first_row, TOK_SHARD, 0)
        k_block = lax.dynamic_slice_in_dim(k_pad, first_row, WIN * TOK_SHARD, 0).astype(jnp.float32)
        v_block = lax.dynamic_slice_in_dim(v_pad, first_row, WIN * TOK_SHARD, 0).astype(jnp.float32)
        k_docs = lax.dynamic_slice_in_dim(doc_pad, first_row, WIN * TOK_SHARD, 0)
        q_pos = first_row + jnp.arange(TOK_SHARD, dtype=jnp.int32)
        k_pos = first_row - lead + jnp.arange(WIN * TOK_SHARD, dtype=jnp.int32)
        allowed = (k_pos[None, :] >= 0) & (k_pos[None, :] <= q_pos[:, None]) & (k_docs[None, :] == q_docs[:, None])
        scores = jnp.einsum('tkgd,skd->kgts', q_block, k_block) * scale
        masked = jnp.where(allowed[None, None], scores, -1e+30)
        top = lax.optimization_barrier(jnp.max(masked, axis=-1, keepdims=True))
        weights_exp = jnp.where(allowed[None, None], jnp.exp(scores - top), 0.0)
        total = lax.optimization_barrier(jnp.sum(weights_exp, axis=-1))
        weights_low = weights_exp.astype(jnp.bfloat16).astype(jnp.float32)
        summed = jnp.einsum('kgts,skd->tkgd', weights_low, v_block)
        result = summed / jnp.transpose(total, (2, 0, 1))[..., None]
        return result.reshape(TOK_SHARD, HEADS * HEAD).astype(jnp.bfloat16)
    attended = lax.map(one_shard, jnp.arange(N_CTX, dtype=jnp.int32)).reshape(TOKENS, HEADS * HEAD)
    group_cols = HEADS * HEAD // N_TP
    mixed = jnp.zeros((TOKENS, D), jnp.float32)
    for group in range(N_TP):
        partial_c = jnp.dot(attended[:, group * group_cols:(group + 1) * group_cols], o_weight[group * group_cols:(group + 1) * group_cols, :], preferred_element_type=jnp.float32)
        partial_c = lax.optimization_barrier(partial_c.astype(jnp.bfloat16))
        mixed = mixed + partial_c.astype(jnp.float32)
    return mixed.astype(jnp.bfloat16)
```

```python
import functools
import math
import jax
import jax.numpy as jnp
from jax import lax
from jax.experimental import pallas as pl
from jax.experimental.pallas import tpu as pltpu
from jax.sharding import Mesh, PartitionSpec as P

HEAD = 128


def rotate(values, positions):
    half_dim = values.shape[-1] // 2
    inv_freq = 500000.0 ** (-(jnp.arange(half_dim, dtype=jnp.float32) * 2.0) / values.shape[-1])
    angles = positions[:, None] * inv_freq[None, :]
    cos_part = jnp.cos(angles)[:, None, :]
    sin_part = jnp.sin(angles)[:, None, :]
    first_half = values[..., :half_dim]
    second_half = values[..., half_dim:]
    return jnp.concatenate(
        [
            first_half * cos_part - second_half * sin_part,
            second_half * cos_part + first_half * sin_part,
        ],
        axis=-1,
    )


def flash_kernel(
    kv_heads, group, chunk, n_b, lo_ref, b_ref, q_ref, kv_ref, docq_ref, dock_ref, out_ref, m_ref, l_ref, acc_ref
):
    rows = q_ref.shape[0]
    tile = pl.program_id(0)
    shard = tile * n_b + b_ref[0]
    first_row = shard * rows
    hi = (first_row + rows - 1) // chunk
    lo = lo_ref[tile]
    scale2 = math.log2(math.e) / math.sqrt(HEAD)
    q_pos = first_row + lax.broadcasted_iota(jnp.int32, (rows, chunk), 0)
    k_rel = lax.broadcasted_iota(jnp.int32, (rows, chunk), 1)
    docq = docq_ref[...]

    def step(c, first):
        start = pl.multiple_of(c * chunk, chunk)
        keys = pl.ds(start, chunk)
        allowed = (k_rel + start <= q_pos) & (dock_ref[:, keys] == docq)
        for kh in range(kv_heads):
            k = kv_ref[keys, kh * HEAD : (kh + 1) * HEAD]
            v = kv_ref[keys, (kv_heads + kh) * HEAD : (kv_heads + kh + 1) * HEAD]
            for g in range(group):
                h = kh * group + g
                q = q_ref[:, h * HEAD : (h + 1) * HEAD]
                s = lax.dot_general(q, k, (((1,), (1,)), ((), ())), preferred_element_type=jnp.float32)
                s = jnp.where(allowed, s * scale2, -1e30)
                top = jnp.max(s, axis=-1, keepdims=True)
                if first:
                    new = top
                else:
                    old = m_ref[h]
                    new = jnp.maximum(old, top)
                e = jnp.exp2(s - new)
                total = jnp.sum(e, axis=-1, keepdims=True)
                prod = jnp.dot(e.astype(jnp.bfloat16), v, preferred_element_type=jnp.float32)
                m_ref[h] = new
                if first:
                    l_ref[h] = total
                    acc_ref[h] = prod
                else:
                    factor = jnp.exp2(old - new)
                    l_ref[h] = l_ref[h] * factor + total
                    acc_ref[h] = acc_ref[h] * factor + prod

    step(hi, True)

    def body(i, _):
        step(hi - 1 - i, False)
        return 0

    lax.fori_loop(0, hi - lo, body, 0)
    for h in range(kv_heads * group):
        out_ref[:, h * HEAD : (h + 1) * HEAD] = (acc_ref[h] / l_ref[h]).astype(jnp.bfloat16)


def flash(q, kv, docq, docs, lo, b, n_a, n_b, kv_heads, group, chunk):
    rows = q.shape[0] // n_a
    heads = kv_heads * group
    keys = kv.shape[0]
    smem = pl.BlockSpec(memory_space=pltpu.SMEM)
    return pl.pallas_call(
        functools.partial(flash_kernel, kv_heads, group, chunk, n_b),
        grid=(n_a,),
        out_shape=jax.ShapeDtypeStruct(q.shape, jnp.bfloat16),
        in_specs=[
            smem,
            smem,
            pl.BlockSpec((rows, heads * HEAD), lambda i: (i, 0)),
            pl.BlockSpec((keys, kv.shape[1]), lambda i: (0, 0)),
            pl.BlockSpec((rows, 1), lambda i: (i, 0)),
            pl.BlockSpec((1, keys), lambda i: (0, 0)),
        ],
        out_specs=pl.BlockSpec((rows, heads * HEAD), lambda i: (i, 0)),
        scratch_shapes=[
            pltpu.VMEM((heads, rows, 1), jnp.float32),
            pltpu.VMEM((heads, rows, 1), jnp.float32),
            pltpu.VMEM((heads, rows, HEAD), jnp.float32),
        ],
        compiler_params=pltpu.CompilerParams(vmem_limit_bytes=40 << 20),
    )(lo, b, q, kv, docq, docs)


def local(n_a, n_b, tokens, norm_gain, doc_ids, q_weight, k_weight, v_weight, o_weight):
    t = tokens.shape[0]
    q_cols, kv_cols = q_weight.shape[1] // n_a, k_weight.shape[1] // n_a
    kv_heads = kv_cols // HEAD
    group = q_cols // kv_cols
    cols = q_cols + 2 * kv_cols
    b = lax.axis_index("b")

    w_local = jnp.concatenate(
        [w.reshape(t if w.shape[0] == t else w.shape[0], n_a, -1) for w in (q_weight, k_weight, v_weight)], axis=2
    ).transpose(1, 0, 2)
    w_rows = w_local.shape[1]
    part = lax.all_to_all(w_local, "a", 0, 0) if n_a > 1 else w_local
    weight = lax.all_gather(part, "b", axis=1).reshape(n_a * n_b * w_rows, cols)

    half = lax.all_gather(tokens, "a", axis=0, tiled=True)
    whole = lax.all_gather(half, "tp", axis=1, tiled=True)
    gain_whole = lax.all_gather(norm_gain, "tp", axis=0, tiled=True)
    docs = lax.all_gather(doc_ids, ("a", "b"), axis=0, tiled=True)

    x_float = whole.astype(jnp.float32)
    mean_sq = jnp.mean(x_float * x_float, axis=-1, keepdims=True)
    normed = (x_float * lax.rsqrt(mean_sq + 1e-05) * gain_whole.astype(jnp.float32)).astype(jnp.bfloat16)
    qkv = jnp.dot(normed, weight, preferred_element_type=jnp.float32)

    rows = n_a * t
    pos = ((jnp.arange(n_a, dtype=jnp.int32) * n_b + b)[:, None] * t + jnp.arange(t, dtype=jnp.int32)[None]).reshape(rows)
    rot = rotate(qkv[:, : q_cols + kv_cols].reshape(rows, -1, HEAD), pos.astype(jnp.float32))
    rot = rot.astype(jnp.bfloat16).reshape(rows, q_cols + kv_cols)
    q_rot = rot[:, :q_cols]
    kv = jnp.concatenate([rot[:, q_cols:], qkv[:, q_cols + kv_cols :].astype(jnp.bfloat16)], axis=1)
    kv = lax.all_gather(kv.reshape(n_a, t, 2 * kv_cols), "b", axis=1).reshape(n_a * n_b * t, 2 * kv_cols)

    docq = lax.dynamic_index_in_dim(docs.reshape(n_a, n_b, t), b, 1, keepdims=False)
    chunk = t * min(4, n_a * n_b)
    lo = jnp.sum((docs[None, :] < docq[:, :1]).astype(jnp.int32), axis=1) // chunk
    attended = flash(
        q_rot, kv, docq.reshape(rows, 1), docs[None], lo, b.astype(jnp.int32)[None], n_a, n_b, kv_heads, group, chunk
    )

    o_whole = lax.all_gather(o_weight, "b", axis=1, tiled=True)
    att_whole = lax.all_gather(attended, "a", axis=1, tiled=True)
    partial = jnp.dot(att_whole, o_whole, preferred_element_type=jnp.float32).astype(jnp.bfloat16)
    if n_a > 1:
        partial = lax.all_to_all(partial.reshape(n_a, t, -1), "a", 0, 0).transpose(1, 0, 2).reshape(t, -1)
    return lax.psum_scatter(partial, "tp", scatter_dimension=1, tiled=True)


def solution(mesh):
    n_ctx, n_tp = mesh.shape["ctx"], mesh.shape["tp"]

    def run(tokens, norm_gain, doc_ids, q_weight, k_weight, v_weight, o_weight):
        n_a = math.gcd(math.gcd(k_weight.shape[1] // n_tp // HEAD, n_ctx), 4)
        n_b = n_ctx // n_a
        grid = Mesh(mesh.devices.reshape(n_a, n_b, n_tp), ("a", "b", "tp"))
        ctx = ("a", "b")
        return jax.shard_map(
            functools.partial(local, n_a, n_b),
            mesh=grid,
            in_specs=(P(ctx, "tp"), P("tp"), P(ctx), P(ctx, "tp"), P(ctx, "tp"), P(ctx, "tp"), P("tp", ctx)),
            out_specs=P(ctx, "tp"),
            check_vma=False,
        )(tokens, norm_gain, doc_ids, q_weight, k_weight, v_weight, o_weight)

    return run
```

```python
import functools
import math
import jax
import jax.numpy as jnp
from jax import lax
from jax.experimental import pallas as pl
from jax.experimental.pallas import tpu as pltpu
from jax.sharding import Mesh, PartitionSpec as P

HEAD = 128


def rotate(values, positions):
    half_dim = values.shape[-1] // 2
    inv_freq = 500000.0 ** (-(jnp.arange(half_dim, dtype=jnp.float32) * 2.0) / values.shape[-1])
    angles = positions[:, None] * inv_freq[None, :]
    cos_part = jnp.cos(angles)[:, None, :]
    sin_part = jnp.sin(angles)[:, None, :]
    first_half = values[..., :half_dim]
    second_half = values[..., half_dim:]
    return jnp.concatenate(
        [
            first_half * cos_part - second_half * sin_part,
            second_half * cos_part + first_half * sin_part,
        ],
        axis=-1,
    )


def flash_kernel(
    kv_heads, group, chunk, n_b, lo_ref, b_ref, q_ref, kv_ref, docq_ref, dock_ref, out_ref, m_ref, l_ref, acc_ref
):
    rows = q_ref.shape[0]
    tile = pl.program_id(0)
    shard = tile * n_b + b_ref[0]
    first_row = shard * rows
    hi = (first_row + rows - 1) // chunk
    lo = lo_ref[tile]
    scale2 = math.log2(math.e) / math.sqrt(HEAD)
    q_pos = first_row + lax.broadcasted_iota(jnp.int32, (rows, chunk), 0)
    k_rel = lax.broadcasted_iota(jnp.int32, (rows, chunk), 1)
    docq = docq_ref[...]

    def step(c, first):
        start = pl.multiple_of(c * chunk, chunk)
        keys = pl.ds(start, chunk)
        allowed = (k_rel + start <= q_pos) & (dock_ref[:, keys] == docq)
        for kh in range(kv_heads):
            k = kv_ref[keys, kh * HEAD : (kh + 1) * HEAD]
            v = kv_ref[keys, (kv_heads + kh) * HEAD : (kv_heads + kh + 1) * HEAD]
            for g in range(group):
                h = kh * group + g
                q = q_ref[:, h * HEAD : (h + 1) * HEAD]
                s = lax.dot_general(q, k, (((1,), (1,)), ((), ())), preferred_element_type=jnp.float32)
                s = jnp.where(allowed, s * scale2, -1e30)
                top = jnp.max(s, axis=-1, keepdims=True)
                if first:
                    new = top
                else:
                    old = m_ref[h]
                    new = jnp.maximum(old, top)
                e = jnp.exp2(s - new)
                total = jnp.sum(e, axis=-1, keepdims=True)
                prod = jnp.dot(e.astype(jnp.bfloat16), v, preferred_element_type=jnp.float32)
                m_ref[h] = new
                if first:
                    l_ref[h] = total
                    acc_ref[h] = prod
                else:
                    factor = jnp.exp2(old - new)
                    l_ref[h] = l_ref[h] * factor + total
                    acc_ref[h] = acc_ref[h] * factor + prod

    step(hi, True)

    def body(i, _):
        step(hi - 1 - i, False)
        return 0

    lax.fori_loop(0, hi - lo, body, 0)
    for h in range(kv_heads * group):
        out_ref[:, h * HEAD : (h + 1) * HEAD] = (acc_ref[h] / l_ref[h]).astype(jnp.bfloat16)


def flash(q, kv, docq, docs, lo, b, n_a, n_b, kv_heads, group, chunk):
    rows = q.shape[0] // n_a
    heads = kv_heads * group
    keys = kv.shape[0]
    smem = pl.BlockSpec(memory_space=pltpu.SMEM)
    return pl.pallas_call(
        functools.partial(flash_kernel, kv_heads, group, chunk, n_b),
        grid=(n_a,),
        out_shape=jax.ShapeDtypeStruct(q.shape, jnp.bfloat16),
        in_specs=[
            smem,
            smem,
            pl.BlockSpec((rows, heads * HEAD), lambda i: (i, 0)),
            pl.BlockSpec((keys, kv.shape[1]), lambda i: (0, 0)),
            pl.BlockSpec((rows, 1), lambda i: (i, 0)),
            pl.BlockSpec((1, keys), lambda i: (0, 0)),
        ],
        out_specs=pl.BlockSpec((rows, heads * HEAD), lambda i: (i, 0)),
        scratch_shapes=[
            pltpu.VMEM((heads, rows, 1), jnp.float32),
            pltpu.VMEM((heads, rows, 1), jnp.float32),
            pltpu.VMEM((heads, rows, HEAD), jnp.float32),
        ],
        compiler_params=pltpu.CompilerParams(vmem_limit_bytes=40 << 20),
    )(lo, b, q, kv, docq, docs)


MESH = pl.DeviceIdType.MESH


def place(n, axis, offset):
    return lax.rem(lax.axis_index(axis) + offset, n)


def greet(sizes):
    barrier = pltpu.get_barrier_semaphore()
    count = 0
    for axis, n in sizes.items():
        for o in range(1, n):
            pl.semaphore_signal(barrier, inc=1, device_id={axis: place(n, axis, o)}, device_id_type=MESH)
            count += 1
    pl.semaphore_wait(barrier, count)


def push(src, dst, send, recv, axis, index):
    return pltpu.make_async_remote_copy(
        src_ref=src, dst_ref=dst, send_sem=send, recv_sem=recv, device_id={axis: index}, device_id_type=MESH
    )


def line(n, own, spot, right_sem, left_sem, recv_sem, handle):
    me = lax.axis_index("a")
    right, left = lax.rem(me + 1, n), lax.rem(me + n - 1, n)

    def to_right(k, src, index):
        return push(src, spot(index), right_sem.at[k], recv_sem.at[index], "a", right)

    def to_left(k, src, index):
        return push(src, spot(index), left_sem.at[k], recv_sem.at[index], "a", left)

    def begin():
        @pl.when(me < n - 1)
        def _():
            to_right(0, own, me).start()

        @pl.when(me > 0)
        def _():
            to_left(0, own, me).start()

    def step(k):
        @pl.when(me >= k)
        def _():
            index = me - k
            to_left(k, spot(index), index).wait_recv()

            @pl.when(me < n - 1)
            def _():
                to_right(k, spot(index), index).start()

            handle(k, 0, index)

        @pl.when(me + k < n)
        def _():
            index = me + k
            to_right(k, spot(index), index).wait_recv()

            @pl.when(me > 0)
            def _():
                to_left(k, spot(index), index).start()

            handle(k, 1, index)

    def end():
        for k in range(n):
            @pl.when((me >= k) & (me < n - 1))
            def _():
                to_right(k, own if k == 0 else spot(me - k), me - k).wait_send()

            @pl.when((me + k < n) & (me > 0))
            def _():
                to_left(k, own if k == 0 else spot(me + k), me + k).wait_send()

    return begin, step, end


def input_kernel(
    n_a, n_b, w_ref, tok_ref, gain_ref, weight_ref, whole_ref, gain_out,
    own_sem, z_send, z_recv, p_send, p_recv, right_sem, left_sem, t_recv, c_send, c_recv, g_send, g_recv,
):
    a, b, c = lax.axis_index("a"), lax.axis_index("b"), lax.axis_index("tp")
    t, width = tok_ref.shape
    other = 1 - c
    greet({"a": n_a, "b": n_b, "tp": 2})

    def spot(index, core=c):
        return whole_ref.at[
            pl.ds(pl.multiple_of(index * t, t), t), pl.ds(pl.multiple_of(core * width, width), width)
        ]

    def gain_spot(core):
        return gain_out.at[:, pl.ds(pl.multiple_of(core * width, width), width)]

    exchange = []
    for o in range(1, n_a):
        to = place(n_a, "a", o)
        exchange.append(push(w_ref.at[to], weight_ref.at[a, b], z_send.at[o - 1], z_recv.at[a], "a", to))
        exchange[-1].start()

    def cross(k, side, index):
        src = tok_ref if k == 0 else spot(index)
        return push(src, spot(index), c_send.at[index], c_recv.at[index], "tp", other)

    begin, step, end = line(
        n_a, tok_ref, spot, right_sem, left_sem, t_recv, lambda k, side, index: cross(k, side, index).start()
    )
    begin()

    def plane(k, o):
        index = place(n_a, "a", k)
        src = w_ref.at[index] if k == 0 else weight_ref.at[index, b]
        return push(
            src, weight_ref.at[index, b], p_send.at[k, o - 1], p_recv.at[index, b], "b", place(n_b, "b", o)
        )

    for o in range(1, n_b):
        plane(0, o).start()
    cross(0, 0, a).start()
    gain = push(gain_ref, gain_spot(c), g_send, g_recv, "tp", other)
    gain.start()
    own = [
        pltpu.make_async_copy(w_ref.at[a], weight_ref.at[a, b], own_sem.at[0]),
        pltpu.make_async_copy(tok_ref, spot(a), own_sem.at[1]),
        pltpu.make_async_copy(gain_ref, gain_spot(c), own_sem.at[2]),
    ]
    for copy in own:
        copy.start()
    for k in range(1, n_a):
        index = place(n_a, "a", k)
        push(
            w_ref.at[index], weight_ref.at[index, b], z_send.at[k - 1], z_recv.at[index], "a", index
        ).wait_recv()
        for o in range(1, n_b):
            plane(k, o).start()
        step(k)
    for k in range(n_a):
        for o in range(1, n_b):
            index, source = place(n_a, "a", k), place(n_b, "b", o)
            push(
                w_ref.at[index], weight_ref.at[index, source], p_send.at[k, o - 1], p_recv.at[index, source], "b", source
            ).wait_recv()
    for index in range(n_a):
        push(spot(index), spot(index, other), c_send.at[index], c_recv.at[index], "tp", other).wait_recv()
    push(gain_ref, gain_spot(other), g_send, g_recv, "tp", other).wait_recv()
    for copy in exchange:
        copy.wait_send()
    for k in range(n_a):
        for o in range(1, n_b):
            plane(k, o).wait_send()
    for index in range(n_a):
        push(spot(index), spot(index), c_send.at[index], c_recv.at[index], "tp", other).wait_send()
    gain.wait_send()
    end()
    for copy in own:
        copy.wait()


def kv_kernel(n_b, kv_ref, out_ref, own_sem, send, recv):
    b = lax.axis_index("b")
    greet({"b": n_b})
    copies = [
        push(kv_ref, out_ref.at[:, b], send.at[o - 1], recv.at[b], "b", place(n_b, "b", o)) for o in range(1, n_b)
    ]
    for copy in copies:
        copy.start()
    own = pltpu.make_async_copy(kv_ref, out_ref.at[:, b], own_sem)
    own.start()
    for o in range(1, n_b):
        source = place(n_b, "b", o)
        push(kv_ref, out_ref.at[:, source], send.at[o - 1], recv.at[source], "b", source).wait_recv()
    for copy in copies:
        copy.wait_send()
    own.wait()


def wide_kernel(n_a, n_b, att_ref, o_ref, att_out, o_out, own_sem, right_sem, left_sem, t_recv, send, recv):
    a, b = lax.axis_index("a"), lax.axis_index("b")
    greet({"a": n_a, "b": n_b})
    width, o_width = att_ref.shape[1], o_ref.shape[1]

    def spot(index):
        return att_out.at[:, pl.ds(pl.multiple_of(index * width, width), width)]

    def o_spot(index):
        return o_out.at[:, pl.ds(pl.multiple_of(index * o_width, o_width), o_width)]

    begin, step, end = line(n_a, att_ref, spot, right_sem, left_sem, t_recv, lambda k, side, index: None)
    begin()
    copies = [
        push(o_ref, o_spot(b), send.at[o - 1], recv.at[b], "b", place(n_b, "b", o)) for o in range(1, n_b)
    ]
    for copy in copies:
        copy.start()
    own = [
        pltpu.make_async_copy(att_ref, spot(a), own_sem.at[0]),
        pltpu.make_async_copy(o_ref, o_spot(b), own_sem.at[1]),
    ]
    for copy in own:
        copy.start()
    for k in range(1, n_a):
        step(k)
    for o in range(1, n_b):
        source = place(n_b, "b", o)
        push(o_ref, o_spot(source), send.at[o - 1], recv.at[source], "b", source).wait_recv()
    for copy in copies:
        copy.wait_send()
    end()
    for copy in own:
        copy.wait()


def final_kernel(
    n_a, part_ref, out_ref, got_ref, sum_ref, x_send, x_recv, o_send, o_recv, own_sem
):
    a, b, c = lax.axis_index("a"), lax.axis_index("b"), lax.axis_index("tp")
    half = n_a // 2
    w = part_ref.shape[2]
    barrier = pltpu.get_barrier_semaphore()
    for o in range(n_a):
        for core in (c, 1 - c) if o else (1 - c,):
            pl.semaphore_signal(
                barrier, inc=1, device_id={"a": place(n_a, "a", o), "tp": core}, device_id_type=MESH
            )
    pl.semaphore_wait(barrier, 2 * n_a - 1)
    swaps = [
        push(part_ref.at[(1 - c) * half + i], got_ref.at[i], x_send.at[i], x_recv.at[i], "tp", 1 - c)
        for i in range(half)
    ]
    for copy in swaps:
        copy.start()
    column = lax.rem(a, half)
    goal_core = a // half

    def spot(index):
        return out_ref.at[:, pl.ds(pl.multiple_of(index * w, w), w)]

    def away(i):
        return pltpu.make_async_remote_copy(
            src_ref=sum_ref.at[i], dst_ref=spot(column), send_sem=o_send.at[i], recv_sem=o_recv.at[column],
            device_id={"a": c * half + i, "tp": goal_core}, device_id_type=MESH,
        )

    def home(i):
        return pltpu.make_async_copy(sum_ref.at[i], spot(column), own_sem)

    for i in range(half):
        swaps[i].wait_recv()
        mine = part_ref[c * half + i].astype(jnp.float32)
        sum_ref[i] = (mine + got_ref[i].astype(jnp.float32)).astype(jnp.bfloat16)
        is_me = (c * half + i == a) & (goal_core == c)

        @pl.when(jnp.logical_not(is_me))
        def _():
            away(i).start()

        @pl.when(is_me)
        def _():
            home(i).start()

    for i in range(half):
        is_me = (c * half + i == a) & (goal_core == c)

        @pl.when(jnp.logical_not(is_me))
        def _():
            away(i).wait_send()

        @pl.when(is_me)
        def _():
            home(i).wait()

    for j in range(half):
        @pl.when(jnp.logical_not((c * half + j == a) & (goal_core == c)))
        def _():
            pltpu.make_async_remote_copy(
                src_ref=sum_ref.at[0], dst_ref=spot(j), send_sem=o_send.at[0], recv_sem=o_recv.at[j],
                device_id={"a": place(n_a, "a", 1)}, device_id_type=MESH,
            ).wait_recv()
    for copy in swaps:
        copy.wait_send()


def remote(kernel, number, out_shape, sems, *args, vmem=False, scratch=()):
    space = pltpu.VMEM if vmem else pl.ANY
    dma = pltpu.SemaphoreType.DMA
    return pl.pallas_call(
        kernel,
        out_shape=out_shape,
        in_specs=[pl.BlockSpec(memory_space=space)] * len(args),
        out_specs=jax.tree.map(lambda _: pl.BlockSpec(memory_space=space), out_shape),
        scratch_shapes=[*scratch, *(dma(n) if n else dma for n in sems)],
        compiler_params=pltpu.CompilerParams(
            collective_id=number, has_side_effects=True, vmem_limit_bytes=32 << 20
        ),
    )(*args)


def bf(*shape):
    return jax.ShapeDtypeStruct(shape, jnp.bfloat16)


def local(n_a, n_b, tokens, norm_gain, doc_ids, q_weight, k_weight, v_weight, o_weight):
    t = tokens.shape[0]
    q_cols, kv_cols = q_weight.shape[1] // n_a, k_weight.shape[1] // n_a
    kv_heads = kv_cols // HEAD
    group = q_cols // kv_cols
    cols = q_cols + 2 * kv_cols
    b = lax.axis_index("b")

    w_local = jnp.concatenate(
        [w.reshape(t if w.shape[0] == t else w.shape[0], n_a, -1) for w in (q_weight, k_weight, v_weight)], axis=2
    ).transpose(1, 0, 2)
    w_rows = w_local.shape[1]
    direct = n_a > 1
    if direct:
        weight, whole, gain_whole = remote(
            functools.partial(input_kernel, n_a, n_b), 1,
            (bf(n_a, n_b, w_rows, cols), bf(n_a * t, 2 * tokens.shape[1]), bf(16, 2 * tokens.shape[1])),
            [(3,), (n_a,), (n_a,), (n_a, n_b), (n_a, n_b), (n_a,), (n_a,), (n_a,), (n_a,), (n_a,), None, None],
            w_local, tokens, jnp.broadcast_to(norm_gain[None], (16, norm_gain.shape[0])),
        )
        gain_whole = gain_whole[0]
    else:
        weight = lax.all_gather(w_local, "b", axis=1)
        whole = lax.all_gather(tokens, "tp", axis=1, tiled=True)
        gain_whole = lax.all_gather(norm_gain, "tp", axis=0, tiled=True)
    weight = weight.reshape(n_a * n_b * w_rows, cols)
    docs = lax.all_gather(doc_ids, ("a", "b"), axis=0, tiled=True)

    x_float = whole.astype(jnp.float32)
    mean_sq = jnp.mean(x_float * x_float, axis=-1, keepdims=True)
    normed = (x_float * lax.rsqrt(mean_sq + 1e-05) * gain_whole.astype(jnp.float32)).astype(jnp.bfloat16)
    qkv = jnp.dot(normed, weight, preferred_element_type=jnp.float32)

    rows = n_a * t
    pos = ((jnp.arange(n_a, dtype=jnp.int32) * n_b + b)[:, None] * t + jnp.arange(t, dtype=jnp.int32)[None]).reshape(rows)
    rot = rotate(qkv[:, : q_cols + kv_cols].reshape(rows, -1, HEAD), pos.astype(jnp.float32))
    rot = rot.astype(jnp.bfloat16).reshape(rows, q_cols + kv_cols)
    q_rot = rot[:, :q_cols]
    kv = jnp.concatenate([rot[:, q_cols:], qkv[:, q_cols + kv_cols :].astype(jnp.bfloat16)], axis=1)
    kv = kv.reshape(n_a, t, 2 * kv_cols)
    if direct:
        kv = remote(
            functools.partial(kv_kernel, n_b), 2, bf(n_a, n_b, t, 2 * kv_cols), [None, (n_b,), (n_b,)], kv
        )
    else:
        kv = lax.all_gather(kv, "b", axis=1)
    kv = kv.reshape(n_a * n_b * t, 2 * kv_cols)

    docq = lax.dynamic_index_in_dim(docs.reshape(n_a, n_b, t), b, 1, keepdims=False)
    chunk = t * min(4, n_a * n_b)
    lo = jnp.sum((docs[None, :] < docq[:, :1]).astype(jnp.int32), axis=1) // chunk
    attended = flash(
        q_rot, kv, docq.reshape(rows, 1), docs[None], lo, b.astype(jnp.int32)[None], n_a, n_b, kv_heads, group, chunk
    )

    if direct:
        att_whole, o_whole = remote(
            functools.partial(wide_kernel, n_a, n_b), 3,
            (bf(rows, n_a * q_cols), bf(o_weight.shape[0], n_b * o_weight.shape[1])),
            [(2,), (n_a,), (n_a,), (n_a,), (n_b,), (n_b,)],
            attended, o_weight,
        )
    else:
        att_whole, o_whole = attended, lax.all_gather(o_weight, "b", axis=1, tiled=True)
    partial = jnp.dot(att_whole, o_whole, preferred_element_type=jnp.float32).astype(jnp.bfloat16)
    if direct:
        half, w = n_a // 2, partial.shape[1]
        return remote(
            functools.partial(final_kernel, n_a), 4, bf(t, half * w),
            [(half,), (half,), (half,), (half,), None],
            partial.reshape(n_a, t, w), vmem=True,
            scratch=(pltpu.VMEM((half, t, w), jnp.bfloat16), pltpu.VMEM((half, t, w), jnp.bfloat16)),
        )
    return lax.psum_scatter(partial, "tp", scatter_dimension=1, tiled=True)


def solution(mesh):
    n_ctx, n_tp = mesh.shape["ctx"], mesh.shape["tp"]

    def run(tokens, norm_gain, doc_ids, q_weight, k_weight, v_weight, o_weight):
        n_a = math.gcd(math.gcd(k_weight.shape[1] // n_tp // HEAD, n_ctx), 4) if n_tp == 2 else 1
        n_b = n_ctx // n_a
        grid = Mesh(mesh.devices.reshape(n_a, n_b, n_tp), ("a", "b", "tp"))
        ctx = ("a", "b")
        return jax.shard_map(
            functools.partial(local, n_a, n_b),
            mesh=grid,
            in_specs=(P(ctx, "tp"), P("tp"), P(ctx), P(ctx, "tp"), P(ctx, "tp"), P(ctx, "tp"), P("tp", ctx)),
            out_specs=P(ctx, "tp"),
            check_vma=False,
        )(tokens, norm_gain, doc_ids, q_weight, k_weight, v_weight, o_weight)

    return run
```

```python
import functools
import math
import jax
import jax.numpy as jnp
from jax import lax
from jax.experimental import pallas as pl
from jax.experimental.pallas import tpu as pltpu
from jax.sharding import Mesh, PartitionSpec as P

HEAD = 128


def rotate(values, positions):
    half_dim = values.shape[-1] // 2
    inv_freq = 500000.0 ** (-(jnp.arange(half_dim, dtype=jnp.float32) * 2.0) / values.shape[-1])
    angles = positions[:, None] * inv_freq[None, :]
    cos_part = jnp.cos(angles)[:, None, :]
    sin_part = jnp.sin(angles)[:, None, :]
    first_half = values[..., :half_dim]
    second_half = values[..., half_dim:]
    return jnp.concatenate(
        [
            first_half * cos_part - second_half * sin_part,
            second_half * cos_part + first_half * sin_part,
        ],
        axis=-1,
    )


def flash_kernel(
    kv_heads, group, chunk, n_b, lo_ref, b_ref, q_ref, kv_ref, docq_ref, dock_ref, out_ref, m_ref, l_ref, acc_ref
):
    rows = q_ref.shape[0]
    tile = pl.program_id(0)
    shard = tile * n_b + b_ref[0]
    first_row = shard * rows
    hi = (first_row + rows - 1) // chunk
    lo = lo_ref[tile]
    scale2 = math.log2(math.e) / math.sqrt(HEAD)
    q_pos = first_row + lax.broadcasted_iota(jnp.int32, (rows, chunk), 0)
    k_rel = lax.broadcasted_iota(jnp.int32, (rows, chunk), 1)
    docq = docq_ref[...]

    def step(c, first):
        start = pl.multiple_of(c * chunk, chunk)
        keys = pl.ds(start, chunk)
        allowed = (k_rel + start <= q_pos) & (dock_ref[:, keys] == docq)
        for kh in range(kv_heads):
            k = kv_ref[keys, kh * HEAD : (kh + 1) * HEAD]
            v = kv_ref[keys, (kv_heads + kh) * HEAD : (kv_heads + kh + 1) * HEAD]
            for g in range(group):
                h = kh * group + g
                q = q_ref[:, h * HEAD : (h + 1) * HEAD]
                s = lax.dot_general(q, k, (((1,), (1,)), ((), ())), preferred_element_type=jnp.float32)
                s = jnp.where(allowed, s * scale2, -1e30)
                top = jnp.max(s, axis=-1, keepdims=True)
                if first:
                    new = top
                else:
                    old = m_ref[h]
                    new = jnp.maximum(old, top)
                e = jnp.exp2(s - new)
                total = jnp.sum(e, axis=-1, keepdims=True)
                prod = jnp.dot(e.astype(jnp.bfloat16), v, preferred_element_type=jnp.float32)
                m_ref[h] = new
                if first:
                    l_ref[h] = total
                    acc_ref[h] = prod
                else:
                    factor = jnp.exp2(old - new)
                    l_ref[h] = l_ref[h] * factor + total
                    acc_ref[h] = acc_ref[h] * factor + prod

    step(hi, True)

    def body(i, _):
        step(hi - 1 - i, False)
        return 0

    lax.fori_loop(0, hi - lo, body, 0)
    for h in range(kv_heads * group):
        out_ref[:, h * HEAD : (h + 1) * HEAD] = (acc_ref[h] / l_ref[h]).astype(jnp.bfloat16)


def flash(q, kv, docq, docs, lo, b, n_a, n_b, kv_heads, group, chunk):
    rows = q.shape[0] // n_a
    heads = kv_heads * group
    keys = kv.shape[0]
    smem = pl.BlockSpec(memory_space=pltpu.SMEM)
    return pl.pallas_call(
        functools.partial(flash_kernel, kv_heads, group, chunk, n_b),
        grid=(n_a,),
        out_shape=jax.ShapeDtypeStruct(q.shape, jnp.bfloat16),
        in_specs=[
            smem,
            smem,
            pl.BlockSpec((rows, heads * HEAD), lambda i: (i, 0)),
            pl.BlockSpec((keys, kv.shape[1]), lambda i: (0, 0)),
            pl.BlockSpec((rows, 1), lambda i: (i, 0)),
            pl.BlockSpec((1, keys), lambda i: (0, 0)),
        ],
        out_specs=pl.BlockSpec((rows, heads * HEAD), lambda i: (i, 0)),
        scratch_shapes=[
            pltpu.VMEM((heads, rows, 1), jnp.float32),
            pltpu.VMEM((heads, rows, 1), jnp.float32),
            pltpu.VMEM((heads, rows, HEAD), jnp.float32),
        ],
        compiler_params=pltpu.CompilerParams(vmem_limit_bytes=40 << 20),
    )(lo, b, q, kv, docq, docs)


MESH = pl.DeviceIdType.MESH


def place(n, axis, offset):
    return lax.rem(lax.axis_index(axis) + offset, n)


def greet(sizes):
    barrier = pltpu.get_barrier_semaphore()
    count = 0
    for axis, n in sizes.items():
        for o in range(1, n):
            pl.semaphore_signal(barrier, inc=1, device_id={axis: place(n, axis, o)}, device_id_type=MESH)
            count += 1
    pl.semaphore_wait(barrier, count)


def push(src, dst, send, recv, axis, index):
    return pltpu.make_async_remote_copy(
        src_ref=src, dst_ref=dst, send_sem=send, recv_sem=recv, device_id={axis: index}, device_id_type=MESH
    )


def line(n, own, spot, right_sem, left_sem, recv_sem, handle):
    me = lax.axis_index("a")
    right, left = lax.rem(me + 1, n), lax.rem(me + n - 1, n)

    def to_right(k, src, index):
        return push(src, spot(index), right_sem.at[k], recv_sem.at[index], "a", right)

    def to_left(k, src, index):
        return push(src, spot(index), left_sem.at[k], recv_sem.at[index], "a", left)

    def begin():
        @pl.when(me < n - 1)
        def _():
            to_right(0, own, me).start()

        @pl.when(me > 0)
        def _():
            to_left(0, own, me).start()

    def step(k):
        @pl.when(me >= k)
        def _():
            index = me - k
            to_left(k, spot(index), index).wait_recv()

            @pl.when(me < n - 1)
            def _():
                to_right(k, spot(index), index).start()

            handle(k, 0, index)

        @pl.when(me + k < n)
        def _():
            index = me + k
            to_right(k, spot(index), index).wait_recv()

            @pl.when(me > 0)
            def _():
                to_left(k, spot(index), index).start()

            handle(k, 1, index)

    def end():
        for k in range(n):
            @pl.when((me >= k) & (me < n - 1))
            def _():
                to_right(k, own if k == 0 else spot(me - k), me - k).wait_send()

            @pl.when((me + k < n) & (me > 0))
            def _():
                to_left(k, own if k == 0 else spot(me + k), me + k).wait_send()

    return begin, step, end


def input_kernel(
    n_a, n_b, w_ref, tok_ref, gain_ref, doc_ref, weight_ref, whole_ref, gain_out, doc_out,
    own_sem, z_send, z_recv, p_send, p_recv, right_sem, left_sem, t_recv, c_send, c_recv, g_send, g_recv, d_send, d_recv,
):
    a, b, c = lax.axis_index("a"), lax.axis_index("b"), lax.axis_index("tp")
    t, width = tok_ref.shape
    other = 1 - c
    greet({"a": n_a, "b": n_b, "tp": 2})

    def spot(index, core=c):
        return whole_ref.at[
            pl.ds(pl.multiple_of(index * t, t), t), pl.ds(pl.multiple_of(core * width, width), width)
        ]

    def gain_spot(core):
        return gain_out.at[:, pl.ds(pl.multiple_of(core * width, width), width)]

    exchange = []
    for o in range(1, n_a):
        to = place(n_a, "a", o)
        exchange.append(push(w_ref.at[to], weight_ref.at[a, b], z_send.at[o - 1], z_recv.at[a], "a", to))
        exchange[-1].start()
        exchange.append(push(doc_ref, doc_out.at[a], d_send.at[o - 1], d_recv.at[a], "a", to))
        exchange[-1].start()

    def cross(k, side, index):
        src = tok_ref if k == 0 else spot(index)
        return push(src, spot(index), c_send.at[index], c_recv.at[index], "tp", other)

    begin, step, end = line(
        n_a, tok_ref, spot, right_sem, left_sem, t_recv, lambda k, side, index: cross(k, side, index).start()
    )
    begin()

    def plane(k, o):
        index = place(n_a, "a", k)
        src = w_ref.at[index] if k == 0 else weight_ref.at[index, b]
        return push(
            src, weight_ref.at[index, b], p_send.at[k, o - 1], p_recv.at[index, b], "b", place(n_b, "b", o)
        )

    for o in range(1, n_b):
        plane(0, o).start()
    cross(0, 0, a).start()
    gain = push(gain_ref, gain_spot(c), g_send, g_recv, "tp", other)
    gain.start()
    own = [
        pltpu.make_async_copy(w_ref.at[a], weight_ref.at[a, b], own_sem.at[0]),
        pltpu.make_async_copy(tok_ref, spot(a), own_sem.at[1]),
        pltpu.make_async_copy(gain_ref, gain_spot(c), own_sem.at[2]),
        pltpu.make_async_copy(doc_ref, doc_out.at[a], own_sem.at[3]),
    ]
    for copy in own:
        copy.start()
    for k in range(1, n_a):
        index = place(n_a, "a", k)
        push(
            w_ref.at[index], weight_ref.at[index, b], z_send.at[k - 1], z_recv.at[index], "a", index
        ).wait_recv()
        for o in range(1, n_b):
            plane(k, o).start()
        step(k)
    for k in range(n_a):
        for o in range(1, n_b):
            index, source = place(n_a, "a", k), place(n_b, "b", o)
            push(
                w_ref.at[index], weight_ref.at[index, source], p_send.at[k, o - 1], p_recv.at[index, source], "b", source
            ).wait_recv()
    for index in range(n_a):
        push(spot(index), spot(index, other), c_send.at[index], c_recv.at[index], "tp", other).wait_recv()
    push(gain_ref, gain_spot(other), g_send, g_recv, "tp", other).wait_recv()
    for k in range(1, n_a):
        index = place(n_a, "a", k)
        push(doc_ref, doc_out.at[index], d_send.at[k - 1], d_recv.at[index], "a", index).wait_recv()
    for copy in exchange:
        copy.wait_send()
    for k in range(n_a):
        for o in range(1, n_b):
            plane(k, o).wait_send()
    for index in range(n_a):
        push(spot(index), spot(index), c_send.at[index], c_recv.at[index], "tp", other).wait_send()
    gain.wait_send()
    end()
    for copy in own:
        copy.wait()


def kv_kernel(n_b, kv_ref, doc_ref, out_ref, doc_out, own_sem, send, recv, d_send, d_recv):
    b = lax.axis_index("b")
    greet({"b": n_b})
    copies = []
    for o in range(1, n_b):
        to = place(n_b, "b", o)
        copies.append(push(kv_ref, out_ref.at[:, b], send.at[o - 1], recv.at[b], "b", to))
        copies.append(push(doc_ref, doc_out.at[:, b], d_send.at[o - 1], d_recv.at[b], "b", to))
    own = [
        pltpu.make_async_copy(kv_ref, out_ref.at[:, b], own_sem.at[0]),
        pltpu.make_async_copy(doc_ref, doc_out.at[:, b], own_sem.at[1]),
    ]
    for copy in copies + own:
        copy.start()
    for o in range(1, n_b):
        source = place(n_b, "b", o)
        push(kv_ref, out_ref.at[:, source], send.at[o - 1], recv.at[source], "b", source).wait_recv()
        push(doc_ref, doc_out.at[:, source], d_send.at[o - 1], d_recv.at[source], "b", source).wait_recv()
    for copy in copies:
        copy.wait_send()
    for copy in own:
        copy.wait()


def wide_kernel(n_a, n_b, att_ref, o_ref, att_out, o_out, own_sem, right_sem, left_sem, t_recv, send, recv):
    a, b = lax.axis_index("a"), lax.axis_index("b")
    greet({"a": n_a, "b": n_b})
    width, o_width = att_ref.shape[1], o_ref.shape[1]

    def spot(index):
        return att_out.at[:, pl.ds(pl.multiple_of(index * width, width), width)]

    def o_spot(index):
        return o_out.at[:, pl.ds(pl.multiple_of(index * o_width, o_width), o_width)]

    begin, step, end = line(n_a, att_ref, spot, right_sem, left_sem, t_recv, lambda k, side, index: None)
    begin()
    copies = [
        push(o_ref, o_spot(b), send.at[o - 1], recv.at[b], "b", place(n_b, "b", o)) for o in range(1, n_b)
    ]
    for copy in copies:
        copy.start()
    own = [
        pltpu.make_async_copy(att_ref, spot(a), own_sem.at[0]),
        pltpu.make_async_copy(o_ref, o_spot(b), own_sem.at[1]),
    ]
    for copy in own:
        copy.start()
    for k in range(1, n_a):
        step(k)
    for o in range(1, n_b):
        source = place(n_b, "b", o)
        push(o_ref, o_spot(source), send.at[o - 1], recv.at[source], "b", source).wait_recv()
    for copy in copies:
        copy.wait_send()
    end()
    for copy in own:
        copy.wait()


def final_kernel(
    n_a, part_ref, out_ref, got_ref, sum_ref, x_send, x_recv, o_send, o_recv, own_sem
):
    a, b, c = lax.axis_index("a"), lax.axis_index("b"), lax.axis_index("tp")
    half = n_a // 2
    w = part_ref.shape[2]
    barrier = pltpu.get_barrier_semaphore()
    for o in range(n_a):
        for core in (c, 1 - c) if o else (1 - c,):
            pl.semaphore_signal(
                barrier, inc=1, device_id={"a": place(n_a, "a", o), "tp": core}, device_id_type=MESH
            )
    pl.semaphore_wait(barrier, 2 * n_a - 1)
    swaps = [
        push(part_ref.at[(1 - c) * half + i], got_ref.at[i], x_send.at[i], x_recv.at[i], "tp", 1 - c)
        for i in range(half)
    ]
    for copy in swaps:
        copy.start()
    column = lax.rem(a, half)
    goal_core = a // half

    def spot(index):
        return out_ref.at[:, pl.ds(pl.multiple_of(index * w, w), w)]

    def away(i):
        return pltpu.make_async_remote_copy(
            src_ref=sum_ref.at[i], dst_ref=spot(column), send_sem=o_send.at[i], recv_sem=o_recv.at[column],
            device_id={"a": c * half + i, "tp": goal_core}, device_id_type=MESH,
        )

    def home(i):
        return pltpu.make_async_copy(sum_ref.at[i], spot(column), own_sem)

    for i in range(half):
        swaps[i].wait_recv()
        mine = part_ref[c * half + i].astype(jnp.float32)
        sum_ref[i] = (mine + got_ref[i].astype(jnp.float32)).astype(jnp.bfloat16)
        is_me = (c * half + i == a) & (goal_core == c)

        @pl.when(jnp.logical_not(is_me))
        def _():
            away(i).start()

        @pl.when(is_me)
        def _():
            home(i).start()

    for i in range(half):
        is_me = (c * half + i == a) & (goal_core == c)

        @pl.when(jnp.logical_not(is_me))
        def _():
            away(i).wait_send()

        @pl.when(is_me)
        def _():
            home(i).wait()

    for j in range(half):
        @pl.when(jnp.logical_not((c * half + j == a) & (goal_core == c)))
        def _():
            pltpu.make_async_remote_copy(
                src_ref=sum_ref.at[0], dst_ref=spot(j), send_sem=o_send.at[0], recv_sem=o_recv.at[j],
                device_id={"a": place(n_a, "a", 1)}, device_id_type=MESH,
            ).wait_recv()
    for copy in swaps:
        copy.wait_send()


def remote(kernel, number, out_shape, sems, *args, vmem=False, scratch=()):
    space = pltpu.VMEM if vmem else pl.ANY
    dma = pltpu.SemaphoreType.DMA
    return pl.pallas_call(
        kernel,
        out_shape=out_shape,
        in_specs=[pl.BlockSpec(memory_space=space)] * len(args),
        out_specs=jax.tree.map(lambda _: pl.BlockSpec(memory_space=space), out_shape),
        scratch_shapes=[*scratch, *(dma(n) if n else dma for n in sems)],
        compiler_params=pltpu.CompilerParams(
            collective_id=number, has_side_effects=True, vmem_limit_bytes=32 << 20
        ),
    )(*args)


def bf(*shape):
    return jax.ShapeDtypeStruct(shape, jnp.bfloat16)


def local(n_a, n_b, tokens, norm_gain, doc_ids, q_weight, k_weight, v_weight, o_weight):
    t = tokens.shape[0]
    q_cols, kv_cols = q_weight.shape[1] // n_a, k_weight.shape[1] // n_a
    kv_heads = kv_cols // HEAD
    group = q_cols // kv_cols
    cols = q_cols + 2 * kv_cols
    b = lax.axis_index("b")

    w_local = jnp.concatenate(
        [w.reshape(t if w.shape[0] == t else w.shape[0], n_a, -1) for w in (q_weight, k_weight, v_weight)], axis=2
    ).transpose(1, 0, 2)
    w_rows = w_local.shape[1]
    direct = n_a > 1
    if direct:
        weight, whole, gain_whole, doc_column = remote(
            functools.partial(input_kernel, n_a, n_b), 1,
            (bf(n_a, n_b, w_rows, cols), bf(n_a * t, 2 * tokens.shape[1]), bf(16, 2 * tokens.shape[1]),
             jax.ShapeDtypeStruct((n_a, 8, t), jnp.int32)),
            [(4,), (n_a,), (n_a,), (n_a, n_b), (n_a, n_b), (n_a,), (n_a,), (n_a,), (n_a,), (n_a,), None, None, (n_a,), (n_a,)],
            w_local, tokens, jnp.broadcast_to(norm_gain[None], (16, norm_gain.shape[0])),
            jnp.broadcast_to(doc_ids[None], (8, t)),
        )
        gain_whole = gain_whole[0]
    else:
        weight = lax.all_gather(w_local, "b", axis=1)
        whole = lax.all_gather(tokens, "tp", axis=1, tiled=True)
        gain_whole = lax.all_gather(norm_gain, "tp", axis=0, tiled=True)
    weight = weight.reshape(n_a * n_b * w_rows, cols)

    x_float = whole.astype(jnp.float32)
    mean_sq = jnp.mean(x_float * x_float, axis=-1, keepdims=True)
    normed = (x_float * lax.rsqrt(mean_sq + 1e-05) * gain_whole.astype(jnp.float32)).astype(jnp.bfloat16)
    qkv = jnp.dot(normed, weight, preferred_element_type=jnp.float32)

    rows = n_a * t
    pos = ((jnp.arange(n_a, dtype=jnp.int32) * n_b + b)[:, None] * t + jnp.arange(t, dtype=jnp.int32)[None]).reshape(rows)
    rot = rotate(qkv[:, : q_cols + kv_cols].reshape(rows, -1, HEAD), pos.astype(jnp.float32))
    rot = rot.astype(jnp.bfloat16).reshape(rows, q_cols + kv_cols)
    q_rot = rot[:, :q_cols]
    kv = jnp.concatenate([rot[:, q_cols:], qkv[:, q_cols + kv_cols :].astype(jnp.bfloat16)], axis=1)
    kv = kv.reshape(n_a, t, 2 * kv_cols)
    if direct:
        kv, docs = remote(
            functools.partial(kv_kernel, n_b), 2,
            (bf(n_a, n_b, t, 2 * kv_cols), jax.ShapeDtypeStruct((n_a, n_b, 8, t), jnp.int32)),
            [(2,), (n_b,), (n_b,), (n_b,), (n_b,)], kv, doc_column,
        )
        docs, docq = docs[:, :, 0].reshape(-1), doc_column[:, 0]
    else:
        docs, docq = lax.all_gather(doc_ids, "b", axis=0, tiled=True), doc_ids[None]
        kv = lax.all_gather(kv, "b", axis=1)
    kv = kv.reshape(n_a * n_b * t, 2 * kv_cols)

    chunk = t * min(4, n_a * n_b)
    lo = jnp.sum((docs[None, :] < docq[:, :1]).astype(jnp.int32), axis=1) // chunk
    attended = flash(
        q_rot, kv, docq.reshape(rows, 1), docs[None], lo, b.astype(jnp.int32)[None], n_a, n_b, kv_heads, group, chunk
    )

    if direct:
        att_whole, o_whole = remote(
            functools.partial(wide_kernel, n_a, n_b), 3,
            (bf(rows, n_a * q_cols), bf(o_weight.shape[0], n_b * o_weight.shape[1])),
            [(2,), (n_a,), (n_a,), (n_a,), (n_b,), (n_b,)],
            attended, o_weight,
        )
    else:
        att_whole, o_whole = attended, lax.all_gather(o_weight, "b", axis=1, tiled=True)
    partial = jnp.dot(att_whole, o_whole, preferred_element_type=jnp.float32).astype(jnp.bfloat16)
    if direct:
        half, w = n_a // 2, partial.shape[1]
        return remote(
            functools.partial(final_kernel, n_a), 4, bf(t, half * w),
            [(half,), (half,), (half,), (half,), None],
            partial.reshape(n_a, t, w), vmem=True,
            scratch=(pltpu.VMEM((half, t, w), jnp.bfloat16), pltpu.VMEM((half, t, w), jnp.bfloat16)),
        )
    return lax.psum_scatter(partial, "tp", scatter_dimension=1, tiled=True)


def solution(mesh):
    n_ctx, n_tp = mesh.shape["ctx"], mesh.shape["tp"]

    def run(tokens, norm_gain, doc_ids, q_weight, k_weight, v_weight, o_weight):
        n_a = math.gcd(math.gcd(k_weight.shape[1] // n_tp // HEAD, n_ctx), 4) if n_tp == 2 else 1
        n_b = n_ctx // n_a
        grid = Mesh(mesh.devices.reshape(n_a, n_b, n_tp), ("a", "b", "tp"))
        ctx = ("a", "b")
        return jax.shard_map(
            functools.partial(local, n_a, n_b),
            mesh=grid,
            in_specs=(P(ctx, "tp"), P("tp"), P(ctx), P(ctx, "tp"), P(ctx, "tp"), P(ctx, "tp"), P("tp", ctx)),
            out_specs=P(ctx, "tp"),
            check_vma=False,
        )(tokens, norm_gain, doc_ids, q_weight, k_weight, v_weight, o_weight)

    return run
```
